32 devices in a mesh: seq: 2 (over x), hist: 8 (over z, y), chan: 2 (over core).
Axes of the slice: x: 2, y: 2, z: 4, core: 2. Of those that a mesh axis runs over, the one named last changes fastest.
Arguments:
- history: bfloat16 [4096, 4096], P(('seq', 'hist'), 'chan'), parts along dimension 0, may hold values from -6 to 6
- filter_taps: bfloat16 [2048, 4096], P('hist', 'chan'), may hold values from -0.125 to 0.125
- gate_values: bfloat16 [512, 4096], P(('seq', 'hist'), 'chan'), parts along dimension 0, may hold values from -6 to 6
- out_weight: bfloat16 [4096, 4096], P('chan', 'hist'), may hold values from -0.09375 to 0.09375
Outputs:
- output: bfloat16 [512, 4096], P(('seq', 'hist', 'chan')), parts along dimension 0
The draws below stay inside these ranges and needn't reach their ends.
There are 2 independent parts, one for each index of `seq`. The reference program is written for one: setup_inputs(seed, part) draws one part's arguments, and reference() takes and returns one part's arrays. A program takes and returns all parts, laid end to end along the dimension named above; an argument that names none is the same for every part. Nothing has to cross between parts.
All inputs are finite; a program needn't handle non-finite values.
Results may differ from the reference program's by a relative error of at most 0.013.
Values may be sent and summed in bfloat16 or wider, within the bound.
No kernel may reach another device: no remote copies, remote signals or barrier semaphores. Data moves between devices by JAX's collectives and lax.ppermute only.
A program may use at most 64 MiB of HBM per device.

```python
import jax
import jax.numpy as jnp
from jax import lax

D = 4096
TB = 256
HIST = 2048


def level_of(own_key, shape, split, low, largest):
    factor_of = 1.0
    for dim, parts in split:
        steps = jax.random.uniform(jax.random.fold_in(jax.random.fold_in(own_key, 6), dim), (parts,), jnp.float32, low / len(split), largest / len(split))
        factor_of = factor_of * jnp.repeat(jnp.exp(steps), shape[dim] // parts).reshape((-1,) + (1,) * (len(shape) - 1 - dim))
    return factor_of


def centred(rng, extent, width, bound, pieces=(), dtype=jnp.bfloat16):
    values = jax.random.normal(rng, extent, jnp.float32) * width
    if len(pieces) > 0:
        values = level_of(rng, extent, pieces, -0.22, 0.18) * values
    return jnp.clip(values, min=-bound, max=bound).astype(dtype)


def setup_inputs(seed: int = 0, part: int = 0) -> dict:
    keys = jax.random.split(jax.random.key(seed), 5)
    part_keys = jax.random.split(jax.random.fold_in(keys[4], part), 5)
    history = centred(part_keys[0], (HIST, D), 1.0, 6.0, ((0, 8), (1, 2)))
    filter_taps = centred(keys[1], (HIST, D), (HIST ** -0.5), 0.125, ((0, 8), (1, 2)))
    gate_values = centred(part_keys[2], (TB, D), 1.0, 6.0, ((0, 8), (1, 2)))
    out_weight = centred(keys[3], (D, D), D ** -0.5, 0.09375, ((0, 2), (1, 8)))
    return dict(history=history, filter_taps=filter_taps, gate_values=gate_values, out_weight=out_weight)


def reference(history, filter_taps, gate_values, out_weight):
    block_width = min(256, D)
    count_blocks = D // block_width
    signal = history.astype(jnp.float32).reshape(HIST, count_blocks, block_width).transpose(1, 0, 2)
    kernel = filter_taps.astype(jnp.float32)[::-1].reshape(HIST, count_blocks, block_width).transpose(1, 0, 2)
    length = 2 * HIST

    def conv_block(pair):
        inputs, taps_block = pair
        spectrum = jnp.fft.rfft(inputs, length, axis=0) * jnp.fft.rfft(taps_block, length, axis=0)
        whole = jnp.fft.irfft(spectrum, length, axis=0)
        return whole[HIST - TB:HIST]

    blocks = lax.map(conv_block, (signal, kernel))
    conv = blocks.transpose(1, 0, 2).reshape(TB, D).astype(jnp.float32)
    gated = (conv * gate_values.astype(jnp.float32)).astype(jnp.bfloat16)
    return jnp.dot(gated, out_weight, preferred_element_type=jnp.float32).astype(jnp.bfloat16)
```

```python
import numpy as np

import jax
import jax.numpy as jnp
from jax import lax
from jax.sharding import PartitionSpec as P

BF16 = jnp.bfloat16
F32 = jnp.float32


def halves(values):
    high = values.astype(jnp.bfloat16)
    return high, (values - high.astype(np.float32)).astype(jnp.bfloat16)


def tables(rows, tokens):
    period = rows + tokens
    orders = 2 * np.arange(period // 2)[:, None] + 1
    angles = (orders * np.arange(rows)[None, :] % (2 * period)) * (np.pi / period)
    forward = np.concatenate([np.cos(angles), np.sin(angles)], 0).astype(np.float32)
    lags = tokens - 1 - np.arange(tokens)
    angles = (orders.T * lags[:, None] % (2 * period)) * (np.pi / period)
    inverse = np.concatenate([np.cos(angles), -np.sin(angles)], 1).astype(np.float32)
    inverse = inverse * np.float32(2.0 / period)
    turn = ((orders * rows) % (2 * period)) * (np.pi / period)
    return halves(forward), halves(inverse), np.cos(turn).astype(np.float32), np.sin(turn).astype(np.float32)


def local(history, filter_taps, gate_values, out_weight):
    rows, channels = history.shape
    owned = gate_values.shape[0]
    seqs, hists, chans = (lax.axis_size(a) for a in ("seq", "hist", "chan"))
    tokens = owned * hists
    px = 2 if seqs % 2 == 0 else 1
    py = 2 if hists % 2 == 0 else 1
    nz = hists // py
    wide = channels // py
    quarter = wide // px
    group = tokens // nz
    sx = lax.axis_index("seq") % px
    y = lax.axis_index("hist") % py
    z = lax.axis_index("hist") // py

    def move(value, dx=0, dz=0, dy=0, wrap=True):
        pairs = []
        for s in range(seqs):
            for h in range(hists):
                to_z = h // py + dz
                if not wrap and not 0 <= to_z < nz:
                    continue
                target = (s ^ dx) * hists + (to_z % nz) * py + ((h % py) ^ dy)
                pairs.append((s * hists + h, target))
        return lax.ppermute(value, ("seq", "hist"), pairs)

    def cut(value, dx, dy):
        start = (y ^ dy) * wide + (sx ^ dx) * quarter
        return lax.dynamic_slice_in_dim(value, start, quarter, 1)

    def ordered(index, values):
        if len(values) == 1:
            return values
        first, second = values
        return [jnp.where(index == 0, first, second), jnp.where(index == 0, second, first)]

    (fwd_high, fwd_low), (inv_high, inv_low), turn_cos, turn_sin = tables(rows, tokens)
    modes = fwd_high.shape[0] // 2

    own_taps = cut(filter_taps, 0, 0)
    pieces = [own_taps] + [move(cut(filter_taps, 0, dy), dy=dy) for dy in range(1, py)]
    taps = ordered(y, pieces)
    taps.append(move(taps[0], dz=-1, wrap=False))

    inputs = []
    for dx in range(px):
        blocks = []
        for dy in range(py):
            piece = cut(history, dx, dy)
            blocks.append(piece if dx == dy == 0 else move(piece, dx=dx, dy=dy))
        inputs.append(ordered(y, blocks))

    gates = [lax.dynamic_slice_in_dim(gate_values, (y ^ dy) * wide, wide, 1) for dy in range(py)]
    gates = ordered(y, [gates[0]] + [move(gates[dy], dy=dy) for dy in range(1, py)])
    gate = jnp.concatenate(gates, 0).astype(F32)

    def transform(block):
        out = jnp.dot(fwd_high, block, preferred_element_type=F32)
        out = out + jnp.dot(fwd_low, block, preferred_element_type=F32)
        return out[:modes], out[modes:]

    own_spec = [transform(block) for block in taps]
    contributions = []
    spec = []
    for j in range(py):
        (a, b), (c, d) = own_spec[j], own_spec[j + 1]
        spec.append((a + turn_cos * c - turn_sin * d, b + turn_cos * d + turn_sin * c))
    for dx in range(px):
        real, imag = 0.0, 0.0
        for j in range(py):
            (tc, ts), (ic, is_) = spec[j], transform(inputs[dx][j])
            real = real + tc * ic + ts * is_
            imag = imag + tc * is_ - ts * ic
        product = jnp.concatenate([real, imag], 0)
        high = product.astype(BF16)
        low = (product - high.astype(F32)).astype(BF16)
        conv = jnp.dot(inv_high, high, preferred_element_type=F32)
        conv = conv + jnp.dot(inv_high, low, preferred_element_type=F32)
        conv = conv + jnp.dot(inv_low, high, preferred_element_type=F32)
        contributions.append(conv)

    sums = []
    for dx in range(px):
        total = 0.0
        for dz in range(nz):
            part = lax.dynamic_slice_in_dim(contributions[dx], (z + dz) % nz * group, group, 0)
            if dx or dz:
                part = move(part.astype(BF16), dx=dx, dz=dz).astype(F32)
            total = total + part
        sums.append(total)
    conv = jnp.concatenate(ordered(sx, sums), 1)
    gated = (conv * gate).astype(BF16)

    along = [gated] + [move(gated, dz=-dz) for dz in range(1, nz)]
    total = 0.0
    for dy in range(py):
        across = [move(v, dy=dy) if dy else v for v in along]
        weight = lax.dynamic_slice_in_dim(out_weight, (y ^ dy) * wide, wide, 0)
        total = total + jnp.dot(jnp.concatenate(across, 0), weight, preferred_element_type=F32)
    total = total.astype(BF16).reshape(nz, group, -1)
    total = jnp.roll(total, z, axis=0).reshape(tokens, -1)
    final = lax.all_to_all(total, ("hist", "chan"), split_axis=0, concat_axis=0, tiled=True)
    share = owned // chans
    final = final.reshape(hists, chans, share, -1).astype(F32).sum(1).astype(BF16)
    return final.transpose(1, 0, 2).reshape(share, -1)


def solution(mesh):
    return jax.shard_map(
        local,
        mesh=mesh,
        in_specs=(
            P(("seq", "hist"), "chan"),
            P("hist", "chan"),
            P(("seq", "hist"), "chan"),
            P("chan", "hist"),
        ),
        out_specs=P(("seq", "hist", "chan"), None),
        check_vma=False,
    )
```

```python
import functools

import numpy as np

import jax
import jax.numpy as jnp
from jax import lax
from jax.experimental import pallas as pl
from jax.experimental.pallas import tpu as pltpu
from jax.sharding import PartitionSpec as P

BF16 = jnp.bfloat16
F32 = jnp.float32
VMEM_BYTES = 16 * 1024 * 1024


def halves(values):
    high = values.astype(jnp.bfloat16)
    return high, (values - high.astype(np.float32)).astype(jnp.bfloat16)


def table_of(rows, tokens):
    period = rows + tokens
    orders = 2 * np.arange(period // 2)[:, None] + 1
    angles = (orders * np.arange(rows)[None, :] % (2 * period)) * (np.pi / period)
    forward = halves(np.concatenate([np.cos(angles), np.sin(angles)], 0).astype(np.float32))
    lags = tokens - 1 - np.arange(tokens)
    angles = (orders.T * lags[:, None] % (2 * period)) * (np.pi / period)
    inverse = np.concatenate([np.cos(angles), -np.sin(angles)], 1).astype(np.float32)
    inverse = halves(inverse * np.float32(2.0 / period))
    return np.concatenate([np.concatenate(forward, 1), np.concatenate(inverse, 0)], 0)


def places(px, py):
    sx = lax.rem(lax.axis_index("seq"), px)
    y = lax.rem(lax.axis_index("hist"), py)
    return sx, y, lax.div(lax.axis_index("hist"), py)


def pick_kernel(px, py, width, history, taps, gates, *refs):
    sx, y, _ = places(px, py)
    outs, sems = refs[:-1], refs[-1]
    rows, owned = history.shape[0], gates.shape[0]
    wide = px * width
    copies = []
    outs = list(outs)

    def copy(source, target):
        copies.append(pltpu.make_async_copy(source, target, sems.at[len(copies)]))
        copies[-1].start()

    def columns(dx, dy):
        start = (y ^ dy) * wide + (sx ^ dx) * width
        return pl.ds(pl.multiple_of(start, width), width)

    for dy in range(1, py):
        copy(taps.at[:, columns(0, dy)], outs.pop(0))
    copy(taps.at[:, columns(0, 0)], outs.pop(0))
    for dx in range(px):
        for dy in range(py):
            if dx or dy:
                copy(history.at[:, columns(dx, dy)], outs.pop(0))
    for dy in range(1, py):
        target = outs.pop(0)
        start = pl.multiple_of((y ^ dy) * wide, wide)
        copy(gates.at[:, pl.ds(start, wide)], target)
    for one in copies:
        one.wait()


def transform(table, values):
    period, rows = table.shape[1], values.shape[0]
    out = jnp.dot(table[:period, :rows], values, preferred_element_type=F32)
    return out + jnp.dot(table[:period, rows : 2 * rows], values, preferred_element_type=F32)


def early_kernel(px, py, tile, table, history, taps, *refs):
    peers, outs = refs[: py - 1], refs[py - 1 :]
    sx, y, _ = places(px, py)
    width = outs[0].shape[1]

    def step(number, _):
        cols = pl.ds(pl.multiple_of(number * tile, tile), tile)
        start = y * px * width + sx * width + number * tile
        own = pl.ds(pl.multiple_of(start, tile), tile)
        values = [history[:, own], taps[:, own]] + [r[:, cols] for r in peers]
        for out, value in zip(outs, values):
            out[:, cols] = transform(table, value)
        return 0

    lax.fori_loop(0, width // tile, step, 0)


def conv_kernel(px, py, nz, tile, table, *refs):
    refs = list(refs)
    own_input = refs.pop(0)
    spectra = [refs.pop(0) for _ in range(py)]
    following = [refs.pop(0) for _ in range(py)]
    inputs = [[None if dx == dy == 0 else refs.pop(0) for dy in range(py)] for dx in range(px)]
    outs = [[refs.pop(0) for _ in range(nz)] for _ in range(px)]
    (conv,) = refs
    _, y, z = places(px, py)
    width = own_input.shape[1]
    period = table.shape[1]
    modes = period // 2
    group = outs[0][0].shape[0]
    tokens = conv.shape[1]
    rows = following[0].shape[0]
    assert 2 * rows == period
    odd = lax.broadcasted_iota(jnp.int32, (modes, tile), 0) % 2
    sign = (1 - 2 * odd).astype(F32)

    def step(number, _):
        cols = pl.ds(pl.multiple_of(number * tile, tile), tile)
        after = following[0][:, cols]
        for d in range(1, py):
            after = jnp.where(y == d, following[d][:, cols], after)
        after = transform(table, after)
        held = [r[:, cols] for r in spectra]
        spec = []
        for dy in range(py):
            value = after if py == 1 else jnp.where(y ^ dy == 0, held[1 - dy], after)
            spec.append(
                (
                    held[dy][:modes] - sign * value[modes:],
                    held[dy][modes:] + sign * value[:modes],
                )
            )
        for dx in range(px):
            real, imag = None, None
            for dy in range(py):
                here = inputs[dx][dy]
                out = own_input[:, cols] if here is None else transform(table, here[:, cols])
                (tc, ts), ic, is_ = spec[dy], out[:modes], out[modes:]
                re, im = tc * ic + ts * is_, tc * is_ - ts * ic
                real, imag = (re, im) if dy == 0 else (real + re, imag + im)
            product = jnp.concatenate([real, imag], 0)
            high = product.astype(BF16)
            low = (product - high.astype(F32)).astype(BF16)
            i_high, i_low = table[period : period + tokens, :], table[period + tokens :, :]
            total = jnp.dot(i_high, high, preferred_element_type=F32)
            total = total + jnp.dot(i_high, low, preferred_element_type=F32)
            total = total + jnp.dot(i_low, high, preferred_element_type=F32)
            conv[dx, :, cols] = total
        return 0

    lax.fori_loop(0, width // tile, step, 0)
    for dx in range(px):
        for dz in range(nz):
            begin = pl.multiple_of(lax.rem(z + dz, nz) * group, group)
            out = outs[dx][dz]
            out[...] = conv[dx, pl.ds(begin, group), :].astype(out.dtype)


def local(history, filter_taps, gate_values, out_weight):
    rows, channels = history.shape
    owned = gate_values.shape[0]
    seqs, hists, chans = (lax.axis_size(a) for a in ("seq", "hist", "chan"))
    tokens = owned * hists
    px = 2 if seqs % 2 == 0 else 1
    py = 2 if hists % 2 == 0 else 1
    nz = hists // py
    wide = channels // py
    width = wide // px
    group = tokens // nz
    sx = lax.axis_index("seq") % px
    y = lax.axis_index("hist") % py
    z = lax.axis_index("hist") // py

    def move(value, dx=0, dz=0, dy=0, wrap=True, only=None):
        pairs = []
        for s in range(seqs):
            for h in range(hists):
                to_z = h // py + dz
                if (not wrap and not 0 <= to_z < nz) or only not in (None, h % py):
                    continue
                target = (s ^ dx) * hists + (to_z % nz) * py + ((h % py) ^ dy)
                pairs.append((s * hists + h, target))
        return lax.ppermute(value, ("seq", "hist"), pairs)

    def ordered(index, values):
        if len(values) == 1:
            return values
        first, second = values
        return [jnp.where(index == 0, first, second), jnp.where(index == 0, second, first)]

    hbm = pl.BlockSpec(memory_space=pltpu.HBM)
    vmem = pl.BlockSpec(memory_space=pltpu.VMEM)
    piece = jax.ShapeDtypeStruct((rows, width), BF16)
    shapes = [piece] * (py + px * py - 1) + [jax.ShapeDtypeStruct((owned, wide), BF16)] * (py - 1)
    picked = list(
        pl.pallas_call(
            functools.partial(pick_kernel, px, py, width),
            out_shape=shapes,
            in_specs=[hbm] * 3,
            out_specs=[vmem] * len(shapes),
            scratch_shapes=[pltpu.SemaphoreType.DMA((len(shapes),))],
        )(history, filter_taps, gate_values)
    )
    peers = [move(picked.pop(0), dy=dy) for dy in range(1, py)]
    following = [picked.pop(0)] + peers
    following = [move(v, dz=-1, wrap=False, only=d) for d, v in enumerate(following)]
    inputs = []
    for dx in range(px):
        for dy in range(py):
            if dx or dy:
                inputs.append(move(picked.pop(0), dx=dx, dy=dy))
    gates = [lax.dynamic_slice_in_dim(gate_values, y * wide, wide, 1)]
    gates = ordered(y, gates + [move(picked.pop(0), dy=dy) for dy in range(1, py)])
    gate = jnp.concatenate(gates, 0).astype(F32)

    table = table_of(rows, tokens)
    tile = 256 if width % 256 == 0 else width
    params = pltpu.CompilerParams(vmem_limit_bytes=VMEM_BYTES)
    flops = 4 * rows * 2 * rows * width
    early = pl.pallas_call(
        functools.partial(early_kernel, px, py, tile),
        out_shape=[jax.ShapeDtypeStruct((rows + tokens, width), F32)] * (py + 1),
        in_specs=[vmem] * (2 + py),
        out_specs=[vmem] * (py + 1),
        compiler_params=params,
        cost_estimate=pl.CostEstimate(flops=3 * flops, bytes_accessed=rows * width * 8, transcendentals=0),
    )(table, history, filter_taps, *peers)
    part = lambda own: jax.ShapeDtypeStruct((group, width), F32 if own else BF16)
    contributions = pl.pallas_call(
        functools.partial(conv_kernel, px, py, nz, tile),
        out_shape=[part(dx == dz == 0) for dx in range(px) for dz in range(nz)],
        in_specs=[vmem] * (1 + 1 + py + py + px * py - 1),
        out_specs=[vmem] * (px * nz),
        scratch_shapes=[pltpu.VMEM((px, tokens, width), F32)],
        compiler_params=params,
        cost_estimate=pl.CostEstimate(flops=7 * flops, bytes_accessed=rows * width * 8, transcendentals=0),
    )(table, *early, *following, *inputs)

    sums = []
    for dx in range(px):
        total = None
        for dz in range(nz):
            value = contributions[dx * nz + dz]
            if dx or dz:
                value = move(value, dx=dx, dz=dz).astype(F32)
            total = value if dz == 0 else total + value
        sums.append(total)
    conv = jnp.concatenate(ordered(sx, sums), 1)
    gated = (conv * gate).astype(BF16)

    along = [gated] + [move(gated, dz=-dz) for dz in range(1, nz)]
    total = 0.0
    for dy in range(py):
        across = [move(v, dy=dy) if dy else v for v in along]
        weight = lax.dynamic_slice_in_dim(out_weight, (y ^ dy) * wide, wide, 0)
        total = total + jnp.dot(jnp.concatenate(across, 0), weight, preferred_element_type=F32)
    total = total.astype(BF16).reshape(nz, group, -1)
    total = jnp.roll(total, z, axis=0).reshape(tokens, -1)
    final = lax.all_to_all(total, ("hist", "chan"), split_axis=0, concat_axis=0, tiled=True)
    share = owned // chans
    final = final.reshape(hists, chans, share, -1).astype(F32).sum(1).astype(BF16)
    return final.transpose(1, 0, 2).reshape(share, -1)


def solution(mesh):
    return jax.shard_map(
        local,
        mesh=mesh,
        in_specs=(
            P(("seq", "hist"), "chan"),
            P("hist", "chan"),
            P(("seq", "hist"), "chan"),
            P("chan", "hist"),
        ),
        out_specs=P(("seq", "hist", "chan"), None),
        check_vma=False,
    )
```

```python
import functools

import numpy as np

import jax
import jax.numpy as jnp
from jax import lax
from jax.experimental import pallas as pl
from jax.experimental.pallas import tpu as pltpu
from jax.sharding import PartitionSpec as P

BF16 = jnp.bfloat16
F32 = jnp.float32
VMEM_BYTES = 16 * 1024 * 1024


def halves(values):
    high = values.astype(jnp.bfloat16)
    return high, (values - high.astype(np.float32)).astype(jnp.bfloat16)


def table_of(rows, tokens):
    period = rows + tokens
    orders = 2 * np.arange(period // 2)[:, None] + 1
    angles = (orders * np.arange(rows)[None, :] % (2 * period)) * (np.pi / period)
    forward = halves(np.concatenate([np.cos(angles), np.sin(angles)], 0).astype(np.float32))
    lags = tokens - 1 - np.arange(tokens)
    angles = (orders.T * lags[:, None] % (2 * period)) * (np.pi / period)
    inverse = np.concatenate([np.cos(angles), -np.sin(angles)], 1).astype(np.float32)
    inverse = halves(inverse * np.float32(2.0 / period))
    return np.concatenate([np.concatenate(forward, 1), np.concatenate(inverse, 0)], 0)


def places(px, py):
    sx = lax.rem(lax.axis_index("seq"), px)
    y = lax.rem(lax.axis_index("hist"), py)
    return sx, y, lax.div(lax.axis_index("hist"), py)


def pick_kernel(px, py, width, history, taps, gates, *refs):
    sx, y, _ = places(px, py)
    outs, sems = refs[:-1], refs[-1]
    rows, owned = history.shape[0], gates.shape[0]
    wide = px * width
    copies = []
    outs = list(outs)

    def copy(source, target):
        copies.append(pltpu.make_async_copy(source, target, sems.at[len(copies)]))
        copies[-1].start()

    def columns(dx, dy):
        start = (y ^ dy) * wide + (sx ^ dx) * width
        return pl.ds(pl.multiple_of(start, width), width)

    for dy in range(1, py):
        copy(taps.at[:, columns(0, dy)], outs.pop(0))
    copy(taps.at[:, columns(0, 0)], outs.pop(0))
    for dx in range(px):
        for dy in range(py):
            if dx or dy:
                copy(history.at[:, columns(dx, dy)], outs.pop(0))
    for dy in range(1, py):
        target = outs.pop(0)
        start = pl.multiple_of((y ^ dy) * wide, wide)
        copy(gates.at[:, pl.ds(start, wide)], target)
    for one in copies:
        one.wait()


def transform(table, values):
    period, rows = table.shape[1], values.shape[0]
    twice = jnp.concatenate([values, values], 0)
    return jnp.dot(table[:period, : 2 * rows], twice, preferred_element_type=F32)


def early_kernel(px, py, tile, table, history, taps, *refs):
    peers, outs = refs[: py - 1], refs[py - 1 :]
    sx, y, _ = places(px, py)
    width = outs[0].shape[1]

    def step(number, _):
        cols = pl.ds(pl.multiple_of(number * tile, tile), tile)
        start = y * px * width + sx * width + number * tile
        own = pl.ds(pl.multiple_of(start, tile), tile)
        values = [history[:, own], taps[:, own]] + [r[:, cols] for r in peers]
        for out, value in zip(outs, values):
            out[:, cols] = transform(table, value)
        return 0

    lax.fori_loop(0, width // tile, step, 0)


def conv_kernel(px, py, nz, tile, table, *refs):
    refs = list(refs)
    own_input = refs.pop(0)
    spectra = [refs.pop(0) for _ in range(py)]
    following = [refs.pop(0) for _ in range(py)]
    inputs = [[None if dx == dy == 0 else refs.pop(0) for dy in range(py)] for dx in range(px)]
    outs = [[refs.pop(0) for _ in range(nz)] for _ in range(px)]
    (conv,) = refs
    _, y, z = places(px, py)
    width = own_input.shape[1]
    period = table.shape[1]
    modes = period // 2
    group = outs[0][0].shape[0]
    tokens = conv.shape[1]
    rows = following[0].shape[0]
    assert 2 * rows == period
    odd = lax.broadcasted_iota(jnp.int32, (modes, tile), 0) % 2
    sign = (1 - 2 * odd).astype(F32)

    def step(number, _):
        cols = pl.ds(pl.multiple_of(number * tile, tile), tile)
        after = following[0][:, cols]
        for d in range(1, py):
            after = jnp.where(y == d, following[d][:, cols], after)
        after = transform(table, after)
        held = [r[:, cols] for r in spectra]
        spec = []
        for dy in range(py):
            value = after if py == 1 else jnp.where(y ^ dy == 0, held[1 - dy], after)
            spec.append(
                (
                    held[dy][:modes] - sign * value[modes:],
                    held[dy][modes:] + sign * value[:modes],
                )
            )
        for dx in range(px):
            real, imag = None, None
            for dy in range(py):
                here = inputs[dx][dy]
                out = own_input[:, cols] if here is None else transform(table, here[:, cols])
                (tc, ts), ic, is_ = spec[dy], out[:modes], out[modes:]
                re, im = tc * ic + ts * is_, tc * is_ - ts * ic
                real, imag = (re, im) if dy == 0 else (real + re, imag + im)
            product = jnp.concatenate([real, imag], 0)
            high = product.astype(BF16)
            low = (product - high.astype(F32)).astype(BF16)
            i_high, i_low = table[period : period + tokens, :], table[period + tokens :, :]
            wide_table = jnp.concatenate([i_high, i_high, i_low], 1)
            stacked = jnp.concatenate([high, low, high], 0)
            conv[dx, :, cols] = jnp.dot(wide_table, stacked, preferred_element_type=F32)
        return 0

    lax.fori_loop(0, width // tile, step, 0)
    for dx in range(px):
        for dz in range(nz):
            begin = pl.multiple_of(lax.rem(z + dz, nz) * group, group)
            out = outs[dx][dz]
            out[...] = conv[dx, pl.ds(begin, group), :].astype(out.dtype)


def local(history, filter_taps, gate_values, out_weight):
    rows, channels = history.shape
    owned = gate_values.shape[0]
    seqs, hists, chans = (lax.axis_size(a) for a in ("seq", "hist", "chan"))
    tokens = owned * hists
    px = 2 if seqs % 2 == 0 else 1
    py = 2 if hists % 2 == 0 else 1
    nz = hists // py
    wide = channels // py
    width = wide // px
    group = tokens // nz
    sx = lax.axis_index("seq") % px
    y = lax.axis_index("hist") % py
    z = lax.axis_index("hist") // py

    def move(value, dx=0, dz=0, dy=0, wrap=True, only=None):
        pairs = []
        for s in range(seqs):
            for h in range(hists):
                to_z = h // py + dz
                if (not wrap and not 0 <= to_z < nz) or only not in (None, h % py):
                    continue
                target = (s ^ dx) * hists + (to_z % nz) * py + ((h % py) ^ dy)
                pairs.append((s * hists + h, target))
        return lax.ppermute(value, ("seq", "hist"), pairs)

    def ordered(index, values):
        if len(values) == 1:
            return values
        first, second = values
        return [jnp.where(index == 0, first, second), jnp.where(index == 0, second, first)]

    hbm = pl.BlockSpec(memory_space=pltpu.HBM)
    vmem = pl.BlockSpec(memory_space=pltpu.VMEM)
    piece = jax.ShapeDtypeStruct((rows, width), BF16)
    shapes = [piece] * (py + px * py - 1) + [jax.ShapeDtypeStruct((owned, wide), BF16)] * (py - 1)
    picked = list(
        pl.pallas_call(
            functools.partial(pick_kernel, px, py, width),
            out_shape=shapes,
            in_specs=[hbm] * 3,
            out_specs=[vmem] * len(shapes),
            scratch_shapes=[pltpu.SemaphoreType.DMA((len(shapes),))],
        )(history, filter_taps, gate_values)
    )
    peers = [move(picked.pop(0), dy=dy) for dy in range(1, py)]
    following = [picked.pop(0)] + peers
    following = [move(v, dz=-1, wrap=False, only=d) for d, v in enumerate(following)]
    inputs = []
    for dx in range(px):
        for dy in range(py):
            if dx or dy:
                inputs.append(move(picked.pop(0), dx=dx, dy=dy))
    gates = [lax.dynamic_slice_in_dim(gate_values, y * wide, wide, 1)]
    gates = ordered(y, gates + [move(picked.pop(0), dy=dy) for dy in range(1, py)])
    gate = jnp.concatenate(gates, 0).astype(F32)

    table = table_of(rows, tokens)
    tile = 256 if width % 256 == 0 else width
    params = pltpu.CompilerParams(vmem_limit_bytes=VMEM_BYTES)
    flops = 4 * rows * 2 * rows * width
    early = pl.pallas_call(
        functools.partial(early_kernel, px, py, tile),
        out_shape=[jax.ShapeDtypeStruct((rows + tokens, width), F32)] * (py + 1),
        in_specs=[vmem] * (2 + py),
        out_specs=[vmem] * (py + 1),
        compiler_params=params,
        cost_estimate=pl.CostEstimate(flops=3 * flops, bytes_accessed=rows * width * 8, transcendentals=0),
    )(table, history, filter_taps, *peers)
    part = lambda own: jax.ShapeDtypeStruct((group, width), F32 if own else BF16)
    contributions = pl.pallas_call(
        functools.partial(conv_kernel, px, py, nz, tile),
        out_shape=[part(dx == dz == 0) for dx in range(px) for dz in range(nz)],
        in_specs=[vmem] * (1 + 1 + py + py + px * py - 1),
        out_specs=[vmem] * (px * nz),
        scratch_shapes=[pltpu.VMEM((px, tokens, width), F32)],
        compiler_params=params,
        cost_estimate=pl.CostEstimate(flops=7 * flops, bytes_accessed=rows * width * 8, transcendentals=0),
    )(table, *early, *following, *inputs)

    sums = []
    for dx in range(px):
        total = None
        for dz in range(nz):
            value = contributions[dx * nz + dz]
            if dx or dz:
                value = move(value, dx=dx, dz=dz).astype(F32)
            total = value if dz == 0 else total + value
        sums.append(total)
    conv = jnp.concatenate(ordered(sx, sums), 1)
    gated = (conv * gate).astype(BF16)

    along = [gated] + [move(gated, dz=-dz) for dz in range(1, nz)]
    total = 0.0
    for dy in range(py):
        across = [move(v, dy=dy) if dy else v for v in along]
        weight = lax.dynamic_slice_in_dim(out_weight, (y ^ dy) * wide, wide, 0)
        total = total + jnp.dot(jnp.concatenate(across, 0), weight, preferred_element_type=F32)
    total = total.astype(BF16).reshape(nz, group, -1)
    total = jnp.roll(total, z, axis=0).reshape(tokens, -1)
    share = owned // chans
    total = total.reshape(hists, chans, share, -1)
    if chans == 2:
        c = lax.axis_index("chan")
        sent = lax.dynamic_index_in_dim(total, 1 - c, 1, keepdims=False)
        kept = lax.dynamic_index_in_dim(total, c, 1, keepdims=False)
        sent = lax.ppermute(sent, "chan", [(0, 1), (1, 0)])
        total = kept.astype(F32) + sent.astype(F32)
    else:
        total = lax.psum_scatter(total.astype(F32), "chan", scatter_dimension=1)
    total = total.astype(BF16).reshape(hists * share, -1)
    final = lax.all_to_all(total, "hist", split_axis=0, concat_axis=0, tiled=True)
    return final.reshape(hists, share, -1).transpose(1, 0, 2).reshape(share, -1)


def solution(mesh):
    return jax.shard_map(
        local,
        mesh=mesh,
        in_specs=(
            P(("seq", "hist"), "chan"),
            P("hist", "chan"),
            P(("seq", "hist"), "chan"),
            P("chan", "hist"),
        ),
        out_specs=P(("seq", "hist", "chan"), None),
        check_vma=False,
    )
```

```python
import functools

import numpy as np

import jax
import jax.numpy as jnp
from jax import lax
from jax.experimental import pallas as pl
from jax.experimental.pallas import tpu as pltpu
from jax.sharding import PartitionSpec as P

BF16 = jnp.bfloat16
F32 = jnp.float32
VMEM_BYTES = 16 * 1024 * 1024


def halves(values):
    high = values.astype(jnp.bfloat16)
    return high, (values - high.astype(np.float32)).astype(jnp.bfloat16)


def table_of(rows, tokens):
    period = rows + tokens
    orders = 2 * np.arange(period // 2)[:, None] + 1
    angles = (orders * np.arange(rows)[None, :] % (2 * period)) * (np.pi / period)
    forward = halves(np.concatenate([np.cos(angles), np.sin(angles)], 0).astype(np.float32))
    lags = tokens - 1 - np.arange(tokens)
    angles = (orders.T * lags[:, None] % (2 * period)) * (np.pi / period)
    inverse = np.concatenate([np.cos(angles), -np.sin(angles)], 1).astype(np.float32)
    inverse = halves(inverse * np.float32(2.0 / period))
    return np.concatenate([np.concatenate(forward, 1), np.concatenate(inverse, 0)], 0)


def places(px, py):
    sx = lax.rem(lax.axis_index("seq"), px)
    y = lax.rem(lax.axis_index("hist"), py)
    return sx, y, lax.div(lax.axis_index("hist"), py)


def pick_kernel(px, py, width, history, taps, gates, *refs):
    sx, y, _ = places(px, py)
    outs, sems = refs[:-1], refs[-1]
    rows, owned = history.shape[0], gates.shape[0]
    wide = px * width
    copies = []
    outs = list(outs)

    def copy(source, target):
        copies.append(pltpu.make_async_copy(source, target, sems.at[len(copies)]))
        copies[-1].start()

    def columns(dx, dy):
        start = (y ^ dy) * wide + (sx ^ dx) * width
        return pl.ds(pl.multiple_of(start, width), width)

    for dy in range(1, py):
        copy(taps.at[:, columns(0, dy)], outs.pop(0))
    copy(taps.at[:, columns(0, 0)], outs.pop(0))
    for dx in range(px):
        for dy in range(py):
            if dx or dy:
                copy(history.at[:, columns(dx, dy)], outs.pop(0))
    for dy in range(1, py):
        target = outs.pop(0)
        start = pl.multiple_of((y ^ dy) * wide, wide)
        copy(gates.at[:, pl.ds(start, wide)], target)
    for one in copies:
        one.wait()


def transform(table, values):
    period, rows = table.shape[1], values.shape[0]
    twice = jnp.concatenate([values, values], 0)
    return jnp.dot(table[:period, : 2 * rows], twice, preferred_element_type=F32)


def early_kernel(px, py, tile, table, history, taps, *refs):
    peers, outs = refs[: py - 1], refs[py - 1 :]
    sx, y, _ = places(px, py)
    width = outs[0].shape[1]

    def step(number, _):
        cols = pl.ds(pl.multiple_of(number * tile, tile), tile)
        start = y * px * width + sx * width + number * tile
        own = pl.ds(pl.multiple_of(start, tile), tile)
        values = [history[:, own], taps[:, own]] + [r[:, cols] for r in peers]
        for out, value in zip(outs, values):
            out[:, cols] = transform(table, value)
        return 0

    lax.fori_loop(0, width // tile, step, 0)


def more_kernel(tile, table, *refs):
    values, outs = refs[: len(refs) // 2], refs[len(refs) // 2 :]

    def step(number, _):
        cols = pl.ds(pl.multiple_of(number * tile, tile), tile)
        for out, value in zip(outs, values):
            out[:, cols] = transform(table, value[:, cols])
        return 0

    lax.fori_loop(0, outs[0].shape[1] // tile, step, 0)


def conv_kernel(px, py, nz, tile, table, *refs):
    refs = list(refs)
    own_input = refs.pop(0)
    spectra = [refs.pop(0) for _ in range(py)]
    following = [refs.pop(0) for _ in range(py)]
    inputs = [[None if dx == dy == 0 else refs.pop(0) for dy in range(py)] for dx in range(px)]
    outs = [[refs.pop(0) for _ in range(nz)] for _ in range(px)]
    (conv,) = refs
    _, y, z = places(px, py)
    width = own_input.shape[1]
    period = table.shape[1]
    modes = period // 2
    group = outs[0][0].shape[0]
    tokens = conv.shape[1]
    rows = following[0].shape[0]
    assert 2 * rows == period
    odd = lax.broadcasted_iota(jnp.int32, (modes, tile), 0) % 2
    sign = (1 - 2 * odd).astype(F32)

    def step(number, _):
        cols = pl.ds(pl.multiple_of(number * tile, tile), tile)
        after = following[0][:, cols]
        for d in range(1, py):
            after = jnp.where(y == d, following[d][:, cols], after)
        after = transform(table, after)
        held = [r[:, cols] for r in spectra]
        spec = []
        for dy in range(py):
            value = after if py == 1 else jnp.where(y ^ dy == 0, held[1 - dy], after)
            spec.append(
                (
                    held[dy][:modes] - sign * value[modes:],
                    held[dy][modes:] + sign * value[:modes],
                )
            )
        for dx in range(px):
            real, imag = None, None
            for dy in range(py):
                here = inputs[dx][dy]
                if here is None:
                    out = own_input[:, cols]
                elif dy == 0:
                    out = here[:, cols]
                else:
                    out = transform(table, here[:, cols])
                (tc, ts), ic, is_ = spec[dy], out[:modes], out[modes:]
                re, im = tc * ic + ts * is_, tc * is_ - ts * ic
                real, imag = (re, im) if dy == 0 else (real + re, imag + im)
            product = jnp.concatenate([real, imag], 0)
            high = product.astype(BF16)
            low = (product - high.astype(F32)).astype(BF16)
            i_high, i_low = table[period : period + tokens, :], table[period + tokens :, :]
            wide_table = jnp.concatenate([i_high, i_high, i_low], 1)
            stacked = jnp.concatenate([high, low, high], 0)
            conv[dx, :, cols] = jnp.dot(wide_table, stacked, preferred_element_type=F32)
        return 0

    lax.fori_loop(0, width // tile, step, 0)
    for dx in range(px):
        for dz in range(nz):
            begin = pl.multiple_of(lax.rem(z + dz, nz) * group, group)
            out = outs[dx][dz]
            out[...] = conv[dx, pl.ds(begin, group), :].astype(out.dtype)


def local(history, filter_taps, gate_values, out_weight):
    rows, channels = history.shape
    owned = gate_values.shape[0]
    seqs, hists, chans = (lax.axis_size(a) for a in ("seq", "hist", "chan"))
    tokens = owned * hists
    px = 2 if seqs % 2 == 0 else 1
    py = 2 if hists % 2 == 0 else 1
    nz = hists // py
    wide = channels // py
    width = wide // px
    group = tokens // nz
    sx = lax.axis_index("seq") % px
    y = lax.axis_index("hist") % py
    z = lax.axis_index("hist") // py

    def move(value, dx=0, dz=0, dy=0, wrap=True, only=None):
        pairs = []
        for s in range(seqs):
            for h in range(hists):
                to_z = h // py + dz
                if (not wrap and not 0 <= to_z < nz) or only not in (None, h % py):
                    continue
                target = (s ^ dx) * hists + (to_z % nz) * py + ((h % py) ^ dy)
                pairs.append((s * hists + h, target))
        return lax.ppermute(value, ("seq", "hist"), pairs)

    def ordered(index, values):
        if len(values) == 1:
            return values
        first, second = values
        return [jnp.where(index == 0, first, second), jnp.where(index == 0, second, first)]

    hbm = pl.BlockSpec(memory_space=pltpu.HBM)
    vmem = pl.BlockSpec(memory_space=pltpu.VMEM)
    piece = jax.ShapeDtypeStruct((rows, width), BF16)
    shapes = [piece] * (py + px * py - 1) + [jax.ShapeDtypeStruct((owned, wide), BF16)] * (py - 1)
    picked = list(
        pl.pallas_call(
            functools.partial(pick_kernel, px, py, width),
            out_shape=shapes,
            in_specs=[hbm] * 3,
            out_specs=[vmem] * len(shapes),
            scratch_shapes=[pltpu.SemaphoreType.DMA((len(shapes),))],
        )(history, filter_taps, gate_values)
    )
    peers = [move(picked.pop(0), dy=dy) for dy in range(1, py)]
    following = [picked.pop(0)] + peers
    following = [move(v, dz=-1, wrap=False, only=d) for d, v in enumerate(following)]
    inputs = []
    for dx in range(px):
        for dy in range(py):
            if dx or dy:
                inputs.append(move(picked.pop(0), dx=dx, dy=dy))
    gates = [lax.dynamic_slice_in_dim(gate_values, y * wide, wide, 1)]
    gates = ordered(y, gates + [move(picked.pop(0), dy=dy) for dy in range(1, py)])
    gate = jnp.concatenate(gates, 0).astype(F32)

    table = table_of(rows, tokens)
    tile = 256 if width % 256 == 0 else width
    params = pltpu.CompilerParams(vmem_limit_bytes=VMEM_BYTES)
    flops = 4 * rows * 2 * rows * width
    early = pl.pallas_call(
        functools.partial(early_kernel, px, py, tile),
        out_shape=[jax.ShapeDtypeStruct((rows + tokens, width), F32)] * (py + 1),
        in_specs=[vmem] * (2 + py),
        out_specs=[vmem] * (py + 1),
        compiler_params=params,
        cost_estimate=pl.CostEstimate(flops=3 * flops, bytes_accessed=rows * width * 8, transcendentals=0),
    )(table, history, filter_taps, *peers)
    for dx in range(1, px):
        whole = jax.ShapeDtypeStruct((rows + tokens, width), F32)
        n = dx * py - 1
        inputs[n] = pl.pallas_call(
            functools.partial(more_kernel, tile),
            out_shape=[whole],
            in_specs=[vmem] * 2,
            out_specs=[vmem],
            compiler_params=params,
            cost_estimate=pl.CostEstimate(flops=flops, bytes_accessed=rows * width * 8, transcendentals=0),
        )(table, inputs[n])[0]
    part = lambda own: jax.ShapeDtypeStruct((group, width), F32 if own else BF16)
    contributions = pl.pallas_call(
        functools.partial(conv_kernel, px, py, nz, tile),
        out_shape=[part(dx == dz == 0) for dx in range(px) for dz in range(nz)],
        in_specs=[vmem] * (1 + 1 + py + py + px * py - 1),
        out_specs=[vmem] * (px * nz),
        scratch_shapes=[pltpu.VMEM((px, tokens, width), F32)],
        compiler_params=params,
        cost_estimate=pl.CostEstimate(flops=7 * flops, bytes_accessed=rows * width * 8, transcendentals=0),
    )(table, *early, *following, *inputs)

    sums = []
    for dx in range(px):
        total = None
        for dz in range(nz):
            value = contributions[dx * nz + dz]
            if dx or dz:
                value = move(value, dx=dx, dz=dz).astype(F32)
            total = value if dz == 0 else total + value
        sums.append(total)
    conv = jnp.concatenate(ordered(sx, sums), 1)
    gated = (conv * gate).astype(BF16)

    along = [gated] + [move(gated, dz=-dz) for dz in range(1, nz)]
    total = 0.0
    for dy in range(py):
        across = [move(v, dy=dy) if dy else v for v in along]
        weight = lax.dynamic_slice_in_dim(out_weight, (y ^ dy) * wide, wide, 0)
        total = total + jnp.dot(jnp.concatenate(across, 0), weight, preferred_element_type=F32)
    total = total.astype(BF16).reshape(nz, group, -1)
    total = jnp.roll(total, z, axis=0).reshape(tokens, -1)
    share = owned // chans
    total = total.reshape(hists, chans, share, -1)
    if chans == 2:
        c = lax.axis_index("chan")
        sent = lax.dynamic_index_in_dim(total, 1 - c, 1, keepdims=False)
        kept = lax.dynamic_index_in_dim(total, c, 1, keepdims=False)
        sent = lax.ppermute(sent, "chan", [(0, 1), (1, 0)])
        total = kept.astype(F32) + sent.astype(F32)
    else:
        total = lax.psum_scatter(total.astype(F32), "chan", scatter_dimension=1)
    total = total.astype(BF16).reshape(hists * share, -1)
    final = lax.all_to_all(total, "hist", split_axis=0, concat_axis=0, tiled=True)
    return final.reshape(hists, share, -1).transpose(1, 0, 2).reshape(share, -1)


def solution(mesh):
    return jax.shard_map(
        local,
        mesh=mesh,
        in_specs=(
            P(("seq", "hist"), "chan"),
            P("hist", "chan"),
            P(("seq", "hist"), "chan"),
            P("chan", "hist"),
        ),
        out_specs=P(("seq", "hist", "chan"), None),
        check_vma=False,
    )
```

```python
import functools

import numpy as np

import jax
import jax.numpy as jnp
from jax import lax
from jax.experimental import pallas as pl
from jax.experimental.pallas import tpu as pltpu
from jax.sharding import PartitionSpec as P

BF16 = jnp.bfloat16
F32 = jnp.float32
VMEM_BYTES = 16 * 1024 * 1024
CUT_BYTES = 52 * 1024 * 1024


def halves(values):
    high = values.astype(jnp.bfloat16)
    return high, (values - high.astype(np.float32)).astype(jnp.bfloat16)


def table_of(rows, tokens):
    period = rows + tokens
    orders = 2 * np.arange(period // 2)[:, None] + 1
    angles = (orders * np.arange(rows)[None, :] % (2 * period)) * (np.pi / period)
    forward = halves(np.concatenate([np.cos(angles), np.sin(angles)], 0).astype(np.float32))
    lags = tokens - 1 - np.arange(tokens)
    angles = (orders.T * lags[:, None] % (2 * period)) * (np.pi / period)
    inverse = np.concatenate([np.cos(angles), -np.sin(angles)], 1).astype(np.float32)
    inverse = halves(inverse * np.float32(2.0 / period))
    return np.concatenate([np.concatenate(forward, 1), np.concatenate(inverse, 0)], 0)


def places(px, py):
    sx = lax.rem(lax.axis_index("seq"), px)
    y = lax.rem(lax.axis_index("hist"), py)
    return sx, y, lax.div(lax.axis_index("hist"), py)


def pick_kernel(px, py, width, history, taps, *refs):
    sx, y, _ = places(px, py)
    outs, sems = refs[:-1], refs[-1]
    wide = px * width
    copies = []
    outs = list(outs)

    def copy(source, target):
        copies.append(pltpu.make_async_copy(source, target, sems.at[len(copies)]))
        copies[-1].start()

    def columns(dx, dy):
        start = (y ^ dy) * wide + (sx ^ dx) * width
        return pl.ds(pl.multiple_of(start, width), width)

    for dy in range(1, py):
        copy(taps.at[:, columns(0, dy)], outs.pop(0))
    copy(taps.at[:, columns(0, 0)], outs.pop(0))
    for dx in range(px):
        for dy in range(py):
            if dx or dy:
                copy(history.at[:, columns(dx, dy)], outs.pop(0))
    for one in copies:
        one.wait()


def transform(table, values):
    period, rows = table.shape[1], values.shape[0]
    twice = jnp.concatenate([values, values], 0)
    return jnp.dot(table[:period, : 2 * rows], twice, preferred_element_type=F32)


def early_kernel(px, py, tile, table, history, taps, gates, *refs):
    peers, outs = refs[: py - 1], refs[py - 1 :]
    sx, y, _ = places(px, py)
    width = outs[0].shape[1]
    for dy in range(1, py):
        start = pl.multiple_of((y ^ dy) * px * width, px * width)
        outs[py + dy][...] = gates[:, pl.ds(start, px * width)]

    def step(number, _):
        cols = pl.ds(pl.multiple_of(number * tile, tile), tile)
        start = y * px * width + sx * width + number * tile
        own = pl.ds(pl.multiple_of(start, tile), tile)
        values = [history[:, own], taps[:, own]] + [r[:, cols] for r in peers]
        for out, value in zip(outs, values):
            out[:, cols] = transform(table, value)
        return 0

    lax.fori_loop(0, width // tile, step, 0)


def more_kernel(tile, table, *refs):
    values, outs = refs[: len(refs) // 2], refs[len(refs) // 2 :]

    def step(number, _):
        cols = pl.ds(pl.multiple_of(number * tile, tile), tile)
        for out, value in zip(outs, values):
            out[:, cols] = transform(table, value[:, cols])
        return 0

    lax.fori_loop(0, outs[0].shape[1] // tile, step, 0)


def conv_kernel(px, py, nz, tile, table, *refs):
    refs = list(refs)
    own_input = refs.pop(0)
    spectra = [refs.pop(0) for _ in range(py)]
    following = [refs.pop(0) for _ in range(py)]
    inputs = [[None if dx == dy == 0 else refs.pop(0) for dy in range(py)] for dx in range(px)]
    outs = [[refs.pop(0) for _ in range(nz)] for _ in range(px)]
    _, y, z = places(px, py)
    width = own_input.shape[1]
    period = table.shape[1]
    modes = period // 2
    group = outs[0][0].shape[0]
    tokens = group * nz
    rows = following[0].shape[0]
    assert 2 * rows == period
    odd = lax.broadcasted_iota(jnp.int32, (modes, tile), 0) % 2
    sign = (1 - 2 * odd).astype(F32)

    def step(number, _):
        cols = pl.ds(pl.multiple_of(number * tile, tile), tile)
        after = following[0][:, cols]
        for d in range(1, py):
            after = jnp.where(y == d, following[d][:, cols], after)
        after = transform(table, after)
        held = [r[:, cols] for r in spectra]
        spec = []
        for dy in range(py):
            value = after if py == 1 else jnp.where(y ^ dy == 0, held[1 - dy], after)
            spec.append(
                (
                    held[dy][:modes] - sign * value[modes:],
                    held[dy][modes:] + sign * value[:modes],
                )
            )
        for dx in range(px):
            real, imag = None, None
            for dy in range(py):
                here = inputs[dx][dy]
                if here is None:
                    out = own_input[:, cols]
                elif dy == 0:
                    out = here[:, cols]
                else:
                    out = transform(table, here[:, cols])
                (tc, ts), ic, is_ = spec[dy], out[:modes], out[modes:]
                re, im = tc * ic + ts * is_, tc * is_ - ts * ic
                real, imag = (re, im) if dy == 0 else (real + re, imag + im)
            product = jnp.concatenate([real, imag], 0)
            high = product.astype(BF16)
            low = (product - high.astype(F32)).astype(BF16)
            rows_of = []
            for dz in range(nz):
                begin = pl.multiple_of(period + lax.rem(z + dz, nz) * group, group)
                i_high, i_low = table[pl.ds(begin, group), :], table[pl.ds(begin + tokens, group), :]
                rows_of.append(jnp.concatenate([i_high, i_high, i_low], 1))
            stacked = jnp.concatenate([high, low, high], 0)
            total = jnp.dot(jnp.concatenate(rows_of, 0), stacked, preferred_element_type=F32)
            for dz in range(nz):
                out = outs[dx][dz]
                out[:, cols] = total[dz * group : (dz + 1) * group].astype(out.dtype)
        return 0

    lax.fori_loop(0, width // tile, step, 0)


def local(history, filter_taps, gate_values, out_weight):
    rows, channels = history.shape
    owned = gate_values.shape[0]
    seqs, hists, chans = (lax.axis_size(a) for a in ("seq", "hist", "chan"))
    tokens = owned * hists
    px = 2 if seqs % 2 == 0 else 1
    py = 2 if hists % 2 == 0 else 1
    nz = hists // py
    wide = channels // py
    width = wide // px
    group = tokens // nz
    sx = lax.axis_index("seq") % px
    y = lax.axis_index("hist") % py
    z = lax.axis_index("hist") // py

    def move(value, dx=0, dz=0, dy=0, wrap=True, only=None):
        pairs = []
        for s in range(seqs):
            for h in range(hists):
                to_z = h // py + dz
                if (not wrap and not 0 <= to_z < nz) or only not in (None, h % py):
                    continue
                target = (s ^ dx) * hists + (to_z % nz) * py + ((h % py) ^ dy)
                pairs.append((s * hists + h, target))
        return lax.ppermute(value, ("seq", "hist"), pairs)

    def ordered(index, values):
        if len(values) == 1:
            return values
        first, second = values
        return [jnp.where(index == 0, first, second), jnp.where(index == 0, second, first)]

    hbm = pl.BlockSpec(memory_space=pltpu.HBM)
    vmem = pl.BlockSpec(memory_space=pltpu.VMEM)
    piece = jax.ShapeDtypeStruct((rows, width), BF16)
    shapes = [piece] * (py + px * py - 1)
    picked = list(
        pl.pallas_call(
            functools.partial(pick_kernel, px, py, width),
            out_shape=shapes,
            in_specs=[hbm] * 2,
            out_specs=[vmem] * len(shapes),
            scratch_shapes=[pltpu.SemaphoreType.DMA((len(shapes),))],
            compiler_params=pltpu.CompilerParams(vmem_limit_bytes=CUT_BYTES),
        )(history, filter_taps)
    )
    peers = [move(picked.pop(0), dy=dy) for dy in range(1, py)]
    following = [picked.pop(0)] + peers
    following = [move(v, dz=-1, wrap=False, only=d) for d, v in enumerate(following)]
    inputs = []
    for dx in range(px):
        for dy in range(py):
            if dx or dy:
                inputs.append(move(picked.pop(0), dx=dx, dy=dy))
    table = table_of(rows, tokens)
    tile = 256 if width % 256 == 0 else width
    params = pltpu.CompilerParams(vmem_limit_bytes=VMEM_BYTES)
    flops = 4 * rows * 2 * rows * width
    early = pl.pallas_call(
        functools.partial(early_kernel, px, py, tile),
        out_shape=[jax.ShapeDtypeStruct((rows + tokens, width), F32)] * (py + 1)
        + [jax.ShapeDtypeStruct((owned, wide), BF16)] * (py - 1),
        in_specs=[vmem] * (3 + py),
        out_specs=[vmem] * (2 * py),
        compiler_params=params,
        cost_estimate=pl.CostEstimate(flops=3 * flops, bytes_accessed=rows * width * 8, transcendentals=0),
    )(table, history, filter_taps, gate_values, *peers)
    gates = [lax.dynamic_slice_in_dim(gate_values, y * wide, wide, 1)]
    gates = ordered(y, gates + [move(v, dy=dy) for dy, v in enumerate(early[py + 1 :], 1)])
    gate = jnp.concatenate(gates, 0).astype(F32)

    early = early[: py + 1]
    for dx in range(1, px):
        whole = jax.ShapeDtypeStruct((rows + tokens, width), F32)
        n = dx * py - 1
        inputs[n] = pl.pallas_call(
            functools.partial(more_kernel, tile),
            out_shape=[whole],
            in_specs=[vmem] * 2,
            out_specs=[vmem],
            compiler_params=params,
            cost_estimate=pl.CostEstimate(flops=flops, bytes_accessed=rows * width * 8, transcendentals=0),
        )(table, inputs[n])[0]
    part = lambda own: jax.ShapeDtypeStruct((group, width), F32 if own else BF16)
    contributions = pl.pallas_call(
        functools.partial(conv_kernel, px, py, nz, tile),
        out_shape=[part(dx == dz == 0) for dx in range(px) for dz in range(nz)],
        in_specs=[vmem] * (1 + 1 + py + py + px * py - 1),
        out_specs=[vmem] * (px * nz),
        compiler_params=params,
        cost_estimate=pl.CostEstimate(flops=7 * flops, bytes_accessed=rows * width * 8, transcendentals=0),
    )(table, *early, *following, *inputs)

    sums = []
    for dx in range(px):
        total = None
        for dz in range(nz):
            value = contributions[dx * nz + dz]
            if dx or dz:
                value = move(value, dx=dx, dz=dz).astype(F32)
            total = value if dz == 0 else total + value
        sums.append(total)
    conv = jnp.concatenate(ordered(sx, sums), 1)
    gated = (conv * gate).astype(BF16)

    along = [gated] + [move(gated, dz=-dz) for dz in range(1, nz)]
    total = 0.0
    for dy in range(py):
        across = [move(v, dy=dy) if dy else v for v in along]
        weight = lax.dynamic_slice_in_dim(out_weight, (y ^ dy) * wide, wide, 0)
        total = total + jnp.dot(jnp.concatenate(across, 0), weight, preferred_element_type=F32)
    total = total.astype(BF16).reshape(nz, group, -1)
    total = jnp.roll(total, z, axis=0).reshape(tokens, -1)
    share = owned // chans
    total = total.reshape(hists, chans, share, -1)
    if chans == 2:
        c = lax.axis_index("chan")
        sent = lax.dynamic_index_in_dim(total, 1 - c, 1, keepdims=False)
        kept = lax.dynamic_index_in_dim(total, c, 1, keepdims=False)
        sent = lax.ppermute(sent, "chan", [(0, 1), (1, 0)])
        total = kept.astype(F32) + sent.astype(F32)
    else:
        total = lax.psum_scatter(total.astype(F32), "chan", scatter_dimension=1)
    total = total.astype(BF16).reshape(hists * share, -1)
    final = lax.all_to_all(total, "hist", split_axis=0, concat_axis=0, tiled=True)
    return final.reshape(hists, share, -1).transpose(1, 0, 2).reshape(share, -1)


def solution(mesh):
    return jax.shard_map(
        local,
        mesh=mesh,
        in_specs=(
            P(("seq", "hist"), "chan"),
            P("hist", "chan"),
            P(("seq", "hist"), "chan"),
            P("chan", "hist"),
        ),
        out_specs=P(("seq", "hist", "chan"), None),
        check_vma=False,
    )
```

```python
import functools

import numpy as np

import jax
import jax.numpy as jnp
from jax import lax
from jax.experimental import pallas as pl
from jax.experimental.pallas import tpu as pltpu
from jax.sharding import PartitionSpec as P

BF16 = jnp.bfloat16
F32 = jnp.float32
VMEM_BYTES = 16 * 1024 * 1024
CUT_BYTES = 52 * 1024 * 1024


def halves(values):
    high = values.astype(jnp.bfloat16)
    return high, (values - high.astype(np.float32)).astype(jnp.bfloat16)


def table_of(rows, tokens):
    period = rows + tokens
    orders = 2 * np.arange(period // 2)[:, None] + 1
    angles = (orders * np.arange(rows)[None, :] % (2 * period)) * (np.pi / period)
    forward = halves(np.concatenate([np.cos(angles), np.sin(angles)], 0).astype(np.float32))
    lags = tokens - 1 - np.arange(tokens)
    angles = (orders.T * lags[:, None] % (2 * period)) * (np.pi / period)
    inverse = np.concatenate([np.cos(angles), -np.sin(angles)], 1).astype(np.float32)
    inverse = halves(inverse * np.float32(2.0 / period))
    return np.concatenate([np.concatenate(forward, 1), np.concatenate(inverse, 0)], 0)


def places(px, py):
    sx = lax.rem(lax.axis_index("seq"), px)
    y = lax.rem(lax.axis_index("hist"), py)
    return sx, y, lax.div(lax.axis_index("hist"), py)


def pick_kernel(px, py, width, history, taps, *refs):
    sx, y, _ = places(px, py)
    outs, sems = refs[:-1], refs[-1]
    wide = px * width
    copies = []
    outs = list(outs)

    def copy(source, target):
        copies.append(pltpu.make_async_copy(source, target, sems.at[len(copies)]))
        copies[-1].start()

    def columns(dx, dy):
        start = (y ^ dy) * wide + (sx ^ dx) * width
        return pl.ds(pl.multiple_of(start, width), width)

    for dy in range(1, py):
        copy(taps.at[:, columns(0, dy)], outs.pop(0))
    copy(taps.at[:, columns(0, 0)], outs.pop(0))
    for dx in range(px):
        for dy in range(py):
            if dx or dy:
                copy(history.at[:, columns(dx, dy)], outs.pop(0))
    for one in copies:
        one.wait()


def transform(table, values):
    period, rows = table.shape[1], values.shape[0]
    twice = jnp.concatenate([values, values], 0)
    return jnp.dot(table[:period, : 2 * rows], twice, preferred_element_type=F32)


def early_kernel(px, py, tile, table, history, taps, gates, *refs):
    peers, outs = refs[: py - 1], refs[py - 1 :]
    sx, y, _ = places(px, py)
    width = outs[0].shape[1]
    for dy in range(1, py):
        start = pl.multiple_of((y ^ dy) * px * width, px * width)
        outs[py + dy][...] = gates[:, pl.ds(start, px * width)]

    def step(number, _):
        cols = pl.ds(pl.multiple_of(number * tile, tile), tile)
        start = y * px * width + sx * width + number * tile
        own = pl.ds(pl.multiple_of(start, tile), tile)
        values = [history[:, own], taps[:, own]] + [r[:, cols] for r in peers]
        for out, value in zip(outs, values):
            out[:, cols] = transform(table, value)
        return 0

    lax.fori_loop(0, width // tile, step, 0)


def more_kernel(tile, table, *refs):
    values, outs = refs[: len(refs) // 2], refs[len(refs) // 2 :]

    def step(number, _):
        cols = pl.ds(pl.multiple_of(number * tile, tile), tile)
        for out, value in zip(outs, values):
            out[:, cols] = transform(table, value[:, cols])
        return 0

    lax.fori_loop(0, outs[0].shape[1] // tile, step, 0)


def conv_kernel(px, py, nz, tile, table, *refs):
    refs = list(refs)
    own_input = refs.pop(0)
    spectra = [refs.pop(0) for _ in range(py)]
    following = [refs.pop(0) for _ in range(py)]
    inputs = [[None if dx == dy == 0 else refs.pop(0) for dy in range(py)] for dx in range(px)]
    outs = [[refs.pop(0) for _ in range(nz)] for _ in range(px)]
    _, y, z = places(px, py)
    width = own_input.shape[1]
    period = table.shape[1]
    modes = period // 2
    group = outs[0][0].shape[0]
    tokens = group * nz
    rows = following[0].shape[0]
    assert 2 * rows == period
    odd = lax.broadcasted_iota(jnp.int32, (modes, tile), 0) % 2
    sign = (1 - 2 * odd).astype(F32)

    def step(number, _):
        cols = pl.ds(pl.multiple_of(number * tile, tile), tile)
        after = following[0][:, cols]
        for d in range(1, py):
            after = jnp.where(y == d, following[d][:, cols], after)
        after = transform(table, after)
        held = [r[:, cols] for r in spectra]
        spec = []
        for dy in range(py):
            value = after if py == 1 else jnp.where(y ^ dy == 0, held[1 - dy], after)
            spec.append(
                (
                    held[dy][:modes] - sign * value[modes:],
                    held[dy][modes:] + sign * value[:modes],
                )
            )
        for dx in range(px):
            real, imag = None, None
            for dy in range(py):
                here = inputs[dx][dy]
                if here is None:
                    out = own_input[:, cols]
                elif dx:
                    out = here[:, cols]
                else:
                    out = transform(table, here[:, cols])
                (tc, ts), ic, is_ = spec[dy], out[:modes], out[modes:]
                re, im = tc * ic + ts * is_, tc * is_ - ts * ic
                real, imag = (re, im) if dy == 0 else (real + re, imag + im)
            product = jnp.concatenate([real, imag], 0)
            high = product.astype(BF16)
            low = (product - high.astype(F32)).astype(BF16)
            rows_of = []
            for dz in range(nz):
                begin = pl.multiple_of(period + lax.rem(z + dz, nz) * group, group)
                i_high, i_low = table[pl.ds(begin, group), :], table[pl.ds(begin + tokens, group), :]
                rows_of.append(jnp.concatenate([i_high, i_high, i_low], 1))
            stacked = jnp.concatenate([high, low, high], 0)
            total = jnp.dot(jnp.concatenate(rows_of, 0), stacked, preferred_element_type=F32)
            for dz in range(nz):
                out = outs[dx][dz]
                out[:, cols] = total[dz * group : (dz + 1) * group].astype(out.dtype)
        return 0

    lax.fori_loop(0, width // tile, step, 0)


def local(history, filter_taps, gate_values, out_weight):
    rows, channels = history.shape
    owned = gate_values.shape[0]
    seqs, hists, chans = (lax.axis_size(a) for a in ("seq", "hist", "chan"))
    tokens = owned * hists
    px = 2 if seqs % 2 == 0 else 1
    py = 2 if hists % 2 == 0 else 1
    nz = hists // py
    wide = channels // py
    width = wide // px
    group = tokens // nz
    sx = lax.axis_index("seq") % px
    y = lax.axis_index("hist") % py
    z = lax.axis_index("hist") // py

    def move(value, dx=0, dz=0, dy=0, wrap=True, only=None):
        pairs = []
        for s in range(seqs):
            for h in range(hists):
                to_z = h // py + dz
                if (not wrap and not 0 <= to_z < nz) or only not in (None, h % py):
                    continue
                target = (s ^ dx) * hists + (to_z % nz) * py + ((h % py) ^ dy)
                pairs.append((s * hists + h, target))
        return lax.ppermute(value, ("seq", "hist"), pairs)

    def ordered(index, values):
        if len(values) == 1:
            return values
        first, second = values
        return [jnp.where(index == 0, first, second), jnp.where(index == 0, second, first)]

    hbm = pl.BlockSpec(memory_space=pltpu.HBM)
    vmem = pl.BlockSpec(memory_space=pltpu.VMEM)
    piece = jax.ShapeDtypeStruct((rows, width), BF16)
    shapes = [piece] * (py + px * py - 1)
    picked = list(
        pl.pallas_call(
            functools.partial(pick_kernel, px, py, width),
            out_shape=shapes,
            in_specs=[hbm] * 2,
            out_specs=[vmem] * len(shapes),
            scratch_shapes=[pltpu.SemaphoreType.DMA((len(shapes),))],
            compiler_params=pltpu.CompilerParams(vmem_limit_bytes=CUT_BYTES),
        )(history, filter_taps)
    )
    peers = [move(picked.pop(0), dy=dy) for dy in range(1, py)]
    following = [picked.pop(0)] + peers
    following = [move(v, dz=-1, wrap=False, only=d) for d, v in enumerate(following)]
    inputs = []
    for dx in range(px):
        for dy in range(py):
            if dx or dy:
                inputs.append(move(picked.pop(0), dx=dx, dy=dy))
    table = table_of(rows, tokens)
    tile = width
    params = pltpu.CompilerParams(vmem_limit_bytes=VMEM_BYTES)
    flops = 4 * rows * 2 * rows * width
    early = pl.pallas_call(
        functools.partial(early_kernel, px, py, tile),
        out_shape=[jax.ShapeDtypeStruct((rows + tokens, width), F32)] * (py + 1)
        + [jax.ShapeDtypeStruct((owned, wide), BF16)] * (py - 1),
        in_specs=[vmem] * (3 + py),
        out_specs=[vmem] * (2 * py),
        compiler_params=params,
        cost_estimate=pl.CostEstimate(flops=3 * flops, bytes_accessed=rows * width * 8, transcendentals=0),
    )(table, history, filter_taps, gate_values, *peers)
    gates = [lax.dynamic_slice_in_dim(gate_values, y * wide, wide, 1)]
    gates = ordered(y, gates + [move(v, dy=dy) for dy, v in enumerate(early[py + 1 :], 1)])
    gate = jnp.concatenate(gates, 0).astype(F32)

    early = early[: py + 1]
    first, count = py - 1, (px - 1) * py
    if count:
        whole = jax.ShapeDtypeStruct((rows + tokens, width), F32)
        inputs[first:] = pl.pallas_call(
            functools.partial(more_kernel, tile),
            out_shape=[whole] * count,
            in_specs=[vmem] * (1 + count),
            out_specs=[vmem] * count,
            compiler_params=params,
            cost_estimate=pl.CostEstimate(flops=flops, bytes_accessed=rows * width * 8, transcendentals=0),
        )(table, *inputs[first:])
    part = lambda own: jax.ShapeDtypeStruct((group, width), F32 if own else BF16)
    contributions = pl.pallas_call(
        functools.partial(conv_kernel, px, py, nz, tile),
        out_shape=[part(dx == dz == 0) for dx in range(px) for dz in range(nz)],
        in_specs=[vmem] * (1 + 1 + py + py + px * py - 1),
        out_specs=[vmem] * (px * nz),
        compiler_params=params,
        cost_estimate=pl.CostEstimate(flops=7 * flops, bytes_accessed=rows * width * 8, transcendentals=0),
    )(table, *early, *following, *inputs)

    sums = []
    for dx in range(px):
        total = None
        for dz in range(nz):
            value = contributions[dx * nz + dz]
            if dx or dz:
                value = move(value, dx=dx, dz=dz).astype(F32)
            total = value if dz == 0 else total + value
        sums.append(total)
    conv = jnp.concatenate(ordered(sx, sums), 1)
    gated = (conv * gate).astype(BF16)

    along = [gated] + [move(gated, dz=-dz) for dz in range(1, nz)]
    total = 0.0
    for dy in range(py):
        across = [move(v, dy=dy) if dy else v for v in along]
        weight = lax.dynamic_slice_in_dim(out_weight, (y ^ dy) * wide, wide, 0)
        total = total + jnp.dot(jnp.concatenate(across, 0), weight, preferred_element_type=F32)
    total = total.astype(BF16).reshape(nz, group, -1)
    total = jnp.roll(total, z, axis=0).reshape(tokens, -1)
    share = owned // chans
    total = total.reshape(hists, chans, share, -1)
    if chans == 2:
        c = lax.axis_index("chan")
        sent = lax.dynamic_index_in_dim(total, 1 - c, 1, keepdims=False)
        kept = lax.dynamic_index_in_dim(total, c, 1, keepdims=False)
        sent = lax.ppermute(sent, "chan", [(0, 1), (1, 0)])
        total = kept.astype(F32) + sent.astype(F32)
    else:
        total = lax.psum_scatter(total.astype(F32), "chan", scatter_dimension=1)
    total = total.astype(BF16).reshape(hists * share, -1)
    final = lax.all_to_all(total, "hist", split_axis=0, concat_axis=0, tiled=True)
    return final.reshape(hists, share, -1).transpose(1, 0, 2).reshape(share, -1)


def solution(mesh):
    return jax.shard_map(
        local,
        mesh=mesh,
        in_specs=(
            P(("seq", "hist"), "chan"),
            P("hist", "chan"),
            P(("seq", "hist"), "chan"),
            P("chan", "hist"),
        ),
        out_specs=P(("seq", "hist", "chan"), None),
        check_vma=False,
    )
```

```python
import functools

import numpy as np

import jax
import jax.numpy as jnp
from jax import lax
from jax.experimental import pallas as pl
from jax.experimental.pallas import tpu as pltpu
from jax.sharding import PartitionSpec as P

BF16 = jnp.bfloat16
F32 = jnp.float32
VMEM_BYTES = 16 * 1024 * 1024
CUT_BYTES = 52 * 1024 * 1024


def halves(values):
    high = values.astype(jnp.bfloat16)
    return high, (values - high.astype(np.float32)).astype(jnp.bfloat16)


def table_of(rows, tokens):
    period = rows + tokens
    orders = 2 * np.arange(period // 2)[:, None] + 1
    angles = (orders * np.arange(rows)[None, :] % (2 * period)) * (np.pi / period)
    forward = halves(np.concatenate([np.cos(angles), np.sin(angles)], 0).astype(np.float32))
    lags = tokens - 1 - np.arange(tokens)
    angles = (orders.T * lags[:, None] % (2 * period)) * (np.pi / period)
    inverse = np.concatenate([np.cos(angles), -np.sin(angles)], 1).astype(np.float32)
    inverse = halves(inverse * np.float32(2.0 / period))
    return np.concatenate([np.concatenate(forward, 1), np.concatenate(inverse, 0)], 0)


def places(px, py):
    sx = lax.rem(lax.axis_index("seq"), px)
    y = lax.rem(lax.axis_index("hist"), py)
    return sx, y, lax.div(lax.axis_index("hist"), py)


def pick_kernel(px, py, width, history, taps, *refs):
    sx, y, _ = places(px, py)
    outs, sems = refs[:-1], refs[-1]
    wide = px * width
    copies = []
    outs = list(outs)

    def copy(source, target):
        copies.append(pltpu.make_async_copy(source, target, sems.at[len(copies)]))
        copies[-1].start()

    def columns(dx, dy):
        start = (y ^ dy) * wide + (sx ^ dx) * width
        return pl.ds(pl.multiple_of(start, width), width)

    for dy in range(1, py):
        copy(taps.at[:, columns(0, dy)], outs.pop(0))
    copy(taps.at[:, columns(0, 0)], outs.pop(0))
    for dx in range(px):
        for dy in range(py):
            if dx or dy:
                copy(history.at[:, columns(dx, dy)], outs.pop(0))
    for one in copies:
        one.wait()


def transform(table, values):
    period, rows = table.shape[1], values.shape[0]
    twice = jnp.concatenate([values, values], 0)
    return jnp.dot(table[:period, : 2 * rows], twice, preferred_element_type=F32)


def early_kernel(px, py, tile, table, history, taps, gates, *refs):
    peers, outs = refs[: py - 1], refs[py - 1 :]
    sx, y, _ = places(px, py)
    width = outs[0].shape[1]
    for dy in range(1, py):
        start = pl.multiple_of((y ^ dy) * px * width, px * width)
        outs[py + dy][...] = gates[:, pl.ds(start, px * width)]

    def step(number, _):
        cols = pl.ds(pl.multiple_of(number * tile, tile), tile)
        start = y * px * width + sx * width + number * tile
        own = pl.ds(pl.multiple_of(start, tile), tile)
        values = [history[:, own], taps[:, own]] + [r[:, cols] for r in peers]
        for out, value in zip(outs, values):
            out[:, cols] = transform(table, value)
        return 0

    lax.fori_loop(0, width // tile, step, 0)


def more_kernel(tile, table, *refs):
    values, outs = refs[: len(refs) // 2], refs[len(refs) // 2 :]

    def step(number, _):
        cols = pl.ds(pl.multiple_of(number * tile, tile), tile)
        for out, value in zip(outs, values):
            out[:, cols] = transform(table, value[:, cols])
        return 0

    lax.fori_loop(0, outs[0].shape[1] // tile, step, 0)


def conv_kernel(px, py, nz, tile, table, *refs):
    refs = list(refs)
    own_input = refs.pop(0)
    spectra = [refs.pop(0) for _ in range(py)]
    following = [refs.pop(0) for _ in range(py)]
    inputs = [[None if dx == dy == 0 else refs.pop(0) for dy in range(py)] for dx in range(px)]
    outs = [[refs.pop(0) for _ in range(nz)] for _ in range(px)]
    _, y, z = places(px, py)
    width = own_input.shape[1]
    period = table.shape[1]
    modes = period // 2
    group = outs[0][0].shape[0]
    tokens = group * nz
    rows = following[0].shape[0]
    assert 2 * rows == period
    odd = lax.broadcasted_iota(jnp.int32, (modes, tile), 0) % 2
    sign = (1 - 2 * odd).astype(F32)

    def step(number, _):
        cols = pl.ds(pl.multiple_of(number * tile, tile), tile)
        after = following[0][:, cols]
        for d in range(1, py):
            after = jnp.where(y == d, following[d][:, cols], after)
        after = transform(table, after)
        held = [r[:, cols] for r in spectra]
        spec = []
        for dy in range(py):
            value = after if py == 1 else jnp.where(y ^ dy == 0, held[1 - dy], after)
            spec.append(
                (
                    held[dy][:modes] - sign * value[modes:],
                    held[dy][modes:] + sign * value[:modes],
                )
            )
        for dx in range(px):
            real, imag = None, None
            for dy in range(py):
                here = inputs[dx][dy]
                if here is None:
                    out = own_input[:, cols]
                elif dx:
                    out = here[:, cols]
                else:
                    out = transform(table, here[:, cols])
                (tc, ts), ic, is_ = spec[dy], out[:modes], out[modes:]
                re, im = tc * ic + ts * is_, tc * is_ - ts * ic
                real, imag = (re, im) if dy == 0 else (real + re, imag + im)
            product = jnp.concatenate([real, imag], 0)
            high = product.astype(BF16)
            low = (product - high.astype(F32)).astype(BF16)
            rows_of = []
            for dz in range(nz):
                begin = pl.multiple_of(period + lax.rem(z + dz, nz) * group, group)
                i_high, i_low = table[pl.ds(begin, group), :], table[pl.ds(begin + tokens, group), :]
                rows_of.append(jnp.concatenate([i_high, i_high, i_low], 1))
            stacked = jnp.concatenate([high, low, high], 0)
            total = jnp.dot(jnp.concatenate(rows_of, 0), stacked, preferred_element_type=F32)
            for dz in range(nz):
                out = outs[dx][dz]
                out[:, cols] = total[dz * group : (dz + 1) * group].astype(out.dtype)
        return 0

    lax.fori_loop(0, width // tile, step, 0)


def local(history, filter_taps, gate_values, out_weight):
    rows, channels = history.shape
    owned = gate_values.shape[0]
    seqs, hists, chans = (lax.axis_size(a) for a in ("seq", "hist", "chan"))
    tokens = owned * hists
    px = 2 if seqs % 2 == 0 else 1
    py = 2 if hists % 2 == 0 else 1
    nz = hists // py
    wide = channels // py
    width = wide // px
    group = tokens // nz
    sx = lax.axis_index("seq") % px
    y = lax.axis_index("hist") % py
    z = lax.axis_index("hist") // py

    def move(value, dx=0, dz=0, dy=0, wrap=True, only=None, pair=False):
        pairs = []
        for s in range(seqs):
            for h in range(hists):
                to_z = (h // py) ^ dz if pair else h // py + dz
                if (not wrap and not 0 <= to_z < nz) or only not in (None, h % py):
                    continue
                target = (s ^ dx) * hists + (to_z % nz) * py + ((h % py) ^ dy)
                pairs.append((s * hists + h, target))
        return lax.ppermute(value, ("seq", "hist"), pairs)

    def ordered(index, values):
        if len(values) == 1:
            return values
        first, second = values
        return [jnp.where(index == 0, first, second), jnp.where(index == 0, second, first)]

    hbm = pl.BlockSpec(memory_space=pltpu.HBM)
    vmem = pl.BlockSpec(memory_space=pltpu.VMEM)
    piece = jax.ShapeDtypeStruct((rows, width), BF16)
    shapes = [piece] * (py + px * py - 1)
    picked = list(
        pl.pallas_call(
            functools.partial(pick_kernel, px, py, width),
            out_shape=shapes,
            in_specs=[hbm] * 2,
            out_specs=[vmem] * len(shapes),
            scratch_shapes=[pltpu.SemaphoreType.DMA((len(shapes),))],
            compiler_params=pltpu.CompilerParams(vmem_limit_bytes=CUT_BYTES),
        )(history, filter_taps)
    )
    peers = [move(picked.pop(0), dy=dy) for dy in range(1, py)]
    following = [picked.pop(0)] + peers
    following = [move(v, dz=-1, wrap=False, only=d) for d, v in enumerate(following)]
    inputs = []
    for dx in range(px):
        for dy in range(py):
            if dx or dy:
                inputs.append(move(picked.pop(0), dx=dx, dy=dy))
    table = table_of(rows, tokens)
    tile = width
    params = pltpu.CompilerParams(vmem_limit_bytes=VMEM_BYTES)
    flops = 4 * rows * 2 * rows * width
    early = pl.pallas_call(
        functools.partial(early_kernel, px, py, tile),
        out_shape=[jax.ShapeDtypeStruct((rows + tokens, width), F32)] * (py + 1)
        + [jax.ShapeDtypeStruct((owned, wide), BF16)] * (py - 1),
        in_specs=[vmem] * (3 + py),
        out_specs=[vmem] * (2 * py),
        compiler_params=params,
        cost_estimate=pl.CostEstimate(flops=3 * flops, bytes_accessed=rows * width * 8, transcendentals=0),
    )(table, history, filter_taps, gate_values, *peers)
    gates = [lax.dynamic_slice_in_dim(gate_values, y * wide, wide, 1)]
    gates = ordered(y, gates + [move(v, dy=dy) for dy, v in enumerate(early[py + 1 :], 1)])
    gate = jnp.concatenate(gates, 0).astype(F32)

    early = early[: py + 1]
    first, count = py - 1, (px - 1) * py
    if count:
        whole = jax.ShapeDtypeStruct((rows + tokens, width), F32)
        inputs[first:] = pl.pallas_call(
            functools.partial(more_kernel, tile),
            out_shape=[whole] * count,
            in_specs=[vmem] * (1 + count),
            out_specs=[vmem] * count,
            compiler_params=params,
            cost_estimate=pl.CostEstimate(flops=flops, bytes_accessed=rows * width * 8, transcendentals=0),
        )(table, *inputs[first:])
    part = lambda own: jax.ShapeDtypeStruct((group, width), F32 if own else BF16)
    contributions = pl.pallas_call(
        functools.partial(conv_kernel, px, py, nz, tile),
        out_shape=[part(dx == dz == 0) for dx in range(px) for dz in range(nz)],
        in_specs=[vmem] * (1 + 1 + py + py + px * py - 1),
        out_specs=[vmem] * (px * nz),
        compiler_params=params,
        cost_estimate=pl.CostEstimate(flops=7 * flops, bytes_accessed=rows * width * 8, transcendentals=0),
    )(table, *early, *following, *inputs)

    sums = []
    for dx in range(px):
        total = None
        for dz in range(nz):
            value = contributions[dx * nz + dz]
            if dx or dz:
                value = move(value, dx=dx, dz=dz).astype(F32)
            total = value if dz == 0 else total + value
        sums.append(total)
    conv = jnp.concatenate(ordered(sx, sums), 1)
    gated = (conv * gate).astype(BF16)

    paired = nz & (nz - 1) == 0
    along = [gated] + [move(gated, dz=dz if paired else -dz, pair=paired) for dz in range(1, nz)]
    total = 0.0
    for dy in range(py):
        across = [move(v, dy=dy) if dy else v for v in along]
        weight = lax.dynamic_slice_in_dim(out_weight, (y ^ dy) * wide, wide, 0)
        total = total + jnp.dot(jnp.concatenate(across, 0), weight, preferred_element_type=F32)
    total = total.astype(BF16).reshape(nz, group, -1)
    if not paired:
        total = jnp.roll(total, z, axis=0)
    for bit in range(nz.bit_length() - 1 if paired else 0):
        both = total.reshape(nz >> (bit + 1), 2, 1 << bit, group, total.shape[-1])
        total = jnp.where((z >> bit) & 1 == 0, both, both[:, ::-1]).reshape(total.shape)
    total = total.reshape(tokens, -1)
    share = owned // chans
    total = total.reshape(hists, chans, share, -1)
    if chans == 2:
        c = lax.axis_index("chan")
        sent = lax.dynamic_index_in_dim(total, 1 - c, 1, keepdims=False)
        kept = lax.dynamic_index_in_dim(total, c, 1, keepdims=False)
        sent = lax.ppermute(sent, "chan", [(0, 1), (1, 0)])
        total = kept.astype(F32) + sent.astype(F32)
    else:
        total = lax.psum_scatter(total.astype(F32), "chan", scatter_dimension=1)
    total = total.astype(BF16).reshape(hists * share, -1)
    final = lax.all_to_all(total, "hist", split_axis=0, concat_axis=0, tiled=True)
    return final.reshape(hists, share, -1).transpose(1, 0, 2).reshape(share, -1)


def solution(mesh):
    return jax.shard_map(
        local,
        mesh=mesh,
        in_specs=(
            P(("seq", "hist"), "chan"),
            P("hist", "chan"),
            P(("seq", "hist"), "chan"),
            P("chan", "hist"),
        ),
        out_specs=P(("seq", "hist", "chan"), None),
        check_vma=False,
    )
```
